32 devices in a mesh: groups: 2 (over y), vocab: 8 (over z, x), tok: 2 (over core).
Axes of the slice: x: 2, y: 2, z: 4, core: 2. Of those that a mesh axis runs over, the one named last changes fastest.
Arguments:
- hid_student: bfloat16 [32, 4096], P(('groups', 'vocab', 'tok')), parts along dimension 0, may hold values from -170 to 170
- teacher_logits: float32 [32, 8192], P(('groups', 'vocab', 'tok')), parts along dimension 0, may hold values from -288 to 288
- token_scale: bfloat16 [32], P(('groups', 'vocab', 'tok')), parts along dimension 0, may hold values from 128 to 1024
- head_student: bfloat16 [4096, 8192], P('tok', 'vocab'), may hold values from -0.09375 to 0.09375
Outputs:
- divergence: float32 [32], P(('groups', 'vocab', 'tok')), parts along dimension 0
- grad_hidden: bfloat16 [32, 4096], P(('groups', 'vocab', 'tok')), parts along dimension 0
The draws below stay inside these ranges and needn't reach their ends.
There are 2 independent parts, one for each index of `groups`. The reference program is written for one: setup_inputs(seed, part) draws one part's arguments, and reference() takes and returns one part's arrays. A program takes and returns all parts, laid end to end along the dimension named above; an argument that names none is the same for every part. Nothing has to cross between parts.
All inputs are finite; a program needn't handle non-finite values.
Results may differ from the reference program's by a relative error of at most 0.0049.
Values may be sent and summed in bfloat16 or wider, within the bound.
A program may use at most 64 MiB of HBM per device.

```python
import math
import jax
import jax.numpy as jnp

DS = 4096
VOCAB = 8192
TOKENS = 16


def draw_hid_student(key, part):
    key = jax.random.fold_in(key, 11)
    first = jax.random.fold_in(key, 0)
    values = jnp.clip(jax.random.normal(first, (TOKENS, DS), jnp.float32) * 3.0, -18.0, 18.0)
    return values.astype(jnp.bfloat16)


def draw_teacher_logits(key, part):
    key = jax.random.fold_in(key, 23)
    first = jax.random.fold_in(key, 0)
    values = jnp.clip(jax.random.normal(first, (TOKENS, VOCAB), jnp.float32) * 3.0, -18.0, 18.0)
    return values.astype(jnp.float32)


def block_scale(key, extent, shards, least, largest):
    def one(dim, blocks):
        heights = jax.random.uniform(jax.random.fold_in(jax.random.fold_in(key, 6), dim), (blocks,), jnp.float32, least / len(shards), largest / len(shards))
        return jnp.repeat(jnp.exp(heights), extent[dim] // blocks).reshape((-1,) + (1,) * (len(extent) - dim - 1))

    gain = one(*shards[0])
    for cut in shards[1:]:
        gain = gain * one(*cut)
    return gain


def bell_draw(stream_key, extent, spread, bound, pieces=(), dtype=jnp.bfloat16):
    values = jax.random.normal(stream_key, extent, jnp.float32) * spread
    if len(pieces) > 0:
        values = block_scale(stream_key, extent, pieces, -0.22, 0.18) * values
    return jnp.clip(values, min=-bound, max=bound).astype(dtype)


def setup_inputs(seed: int = 0, part: int = 0) -> dict:
    key_of = jax.random.split(jax.random.key(seed), 5)
    part_splits = jax.random.split(jax.random.fold_in(key_of[4], part), 5)
    return {
        "hid_student": draw_hid_student(jax.random.fold_in(jax.random.fold_in(key_of[4], part), 71), part),
        "teacher_logits": draw_teacher_logits(jax.random.fold_in(jax.random.fold_in(key_of[4], part), 71), part),
        "token_scale": jnp.clip(jnp.exp(math.log(1024.0) - 2.0794415 * jax.random.uniform(part_splits[2], (TOKENS,), jnp.float32) ** block_scale(part_splits[2], (TOKENS,), ((0, 16),), -0.2, 0.2)), 128.0, 1024.0).astype(jnp.bfloat16),
        "head_student": bell_draw(key_of[3], (DS, VOCAB), DS ** -0.5, 0.09375, ((0, 2), (1, 8))),
    }


def reference(hid_student, teacher_logits, token_scale, head_student):
    student = jnp.dot(hid_student, head_student, preferred_element_type=jnp.float32)
    teacher = teacher_logits.astype(jnp.float32)
    logp = student - jax.nn.logsumexp(student, axis=1, keepdims=True)
    logq = teacher - jax.nn.logsumexp(teacher, axis=1, keepdims=True)
    logm = jnp.logaddexp(logp, logq) + jnp.log(jnp.float32(0.5))
    prob_p = jnp.exp(logp)
    prob_q = jnp.exp(logq)
    kl_p = jnp.sum(prob_p * (logp - logm), axis=1)
    kl_q = jnp.sum(prob_q * (logq - logm), axis=1)
    divergence = 0.5 * kl_p + 0.5 * kl_q
    scales = token_scale.astype(jnp.float32)[:, None]
    grad_logits = (scales * prob_p * 0.5 * (logp - logm - kl_p[:, None])).astype(jnp.bfloat16)
    grad_hidden = jnp.dot(grad_logits, head_student.T, preferred_element_type=jnp.float32)
    return divergence, grad_hidden.astype(jnp.bfloat16)
```

```python
import functools
import math

import jax
import jax.numpy as jnp
from jax import lax
from jax.experimental import pallas as pl
from jax.experimental.pallas import tpu as pltpu
from jax.sharding import PartitionSpec as P

LANES = 128


def kernel(
    nv,
    hid,
    teach,
    scale,
    head,
    loss,
    grad,
    w,
    hid_in,
    hid_f,
    part,
    rows,
    g_out,
    g_in,
    back_f,
    back,
    back_in,
    w_sems,
    send_sems,
    recv_sems,
):
    tokens = 2 * nv
    depth, cols = head.shape
    hb = depth // LANES
    vb = cols // LANES
    v = lax.axis_index("vocab")
    t = lax.axis_index("tok")
    me = 2 * v + t
    slot = t * nv + v

    chunks = 4
    step = depth // chunks

    def w_copy(c):
        part_of = pl.ds(c * step, step)
        return pltpu.make_async_copy(head.at[part_of], w.at[part_of], w_sems.at[c])

    for c in range(chunks):
        w_copy(c).start()

    def each_peer(fn):
        def one(k, _):
            peer = lax.rem(me + k, tokens)
            fn(peer, peer // 2, lax.rem(peer, 2))
            return 0

        lax.fori_loop(1, tokens, one, 0, unroll=tokens <= 16)

    barrier = pltpu.get_barrier_semaphore()

    def greet(peer, pv, pt):
        pl.semaphore_signal(barrier, inc=1, device_id={"vocab": pv, "tok": pt})

    each_peer(greet)
    pl.semaphore_wait(barrier, tokens - 1)

    def send(phase, src_of, dst):
        def one(peer, pv, pt):
            pltpu.make_async_remote_copy(
                src_ref=src_of(peer, pv, pt),
                dst_ref=dst,
                send_sem=send_sems.at[phase],
                recv_sem=recv_sems.at[phase],
                device_id={"vocab": pv, "tok": pt},
            ).start()

        each_peer(one)

    def wait(sems, phase, buf, block):
        ref = buf.at[pl.ds(0, (tokens - 1) * block)]
        pltpu.make_async_copy(ref, ref, sems.at[phase]).wait()

    def block(i, size):
        return pl.ds(pl.multiple_of(i * size, size), size)

    send(0, lambda p, pv, pt: hid.at[block(pt, hb)], hid_in.at[block(me, hb)])
    hid_in[block(me, hb), :] = hid[block(t, hb), :]

    teacher = teach[...]
    top_t = jnp.max(teacher, keepdims=True)
    logq = teacher - (top_t + jnp.log(jnp.sum(jnp.exp(teacher - top_t), keepdims=True)))

    wait(recv_sems, 0, hid_in, hb)
    hid_f[...] = hid_in[...].astype(jnp.float32)
    x = jnp.concatenate(
        [hid_f[pl.ds(r, tokens, stride=hb), :].astype(jnp.bfloat16) for r in range(hb)], axis=1
    )
    for c in range(chunks):
        w_copy(c).wait()
    wide = 2 * LANES
    for c in range(cols // wide):
        y = jnp.dot(x, w[:, c * wide : (c + 1) * wide], preferred_element_type=jnp.float32)
        for h in range(2):
            part[pl.ds(2 * c + h, tokens, stride=vb), :] = y[:, h * LANES : (h + 1) * LANES]

    send(1, lambda p, pv, pt: part.at[block(p, vb)], rows.at[block(slot, vb)])
    rows[block(slot, vb), :] = part[block(me, vb), :]
    wait(recv_sems, 1, rows, vb)
    student = rows[0 : nv * vb, :] + rows[nv * vb : 2 * nv * vb, :]

    top_s = jnp.max(student, keepdims=True)
    logp = student - (top_s + jnp.log(jnp.sum(jnp.exp(student - top_s), keepdims=True)))
    logm = (
        jnp.maximum(logp, logq)
        + jnp.log1p(jnp.exp(-jnp.abs(logp - logq)))
        + jnp.float32(math.log(0.5))
    )
    prob_p = jnp.exp(logp)
    diff_p = logp - logm
    kl_p = jnp.sum(prob_p * diff_p, keepdims=True)
    weight = scale[...].astype(jnp.float32)
    g = (weight * prob_p * 0.5 * (diff_p - kl_p)).astype(jnp.bfloat16)
    g_out[...] = g.astype(jnp.float32)

    send(2, lambda p, pv, pt: g_out.at[block(pv, vb)], g_in.at[block(me, vb)])
    g_in[block(me, vb), :] = g_out[block(v, vb), :]
    kl_q = jnp.sum(jnp.exp(logq) * (logq - logm), keepdims=True)
    loss[...] = jnp.broadcast_to(0.5 * kl_p + 0.5 * kl_q, loss.shape)

    wait(recv_sems, 2, g_in, vb)
    gl = jnp.concatenate(
        [g_in[pl.ds(j, tokens, stride=vb), :].astype(jnp.bfloat16) for j in range(vb)], axis=1
    )
    for c in range(depth // wide):
        y = lax.dot_general(
            gl,
            w[c * wide : (c + 1) * wide, :],
            (((1,), (1,)), ((), ())),
            preferred_element_type=jnp.float32,
        )
        for h in range(2):
            back_f[pl.ds(2 * c + h, tokens, stride=hb), :] = y[:, h * LANES : (h + 1) * LANES]
    back[...] = back_f[...].astype(jnp.bfloat16)

    send(3, lambda p, pv, pt: back.at[block(p, hb)], back_in.at[block(slot, hb)])
    back_in[block(slot, hb), :] = back[block(me, hb), :]
    wait(recv_sems, 3, back_in, hb)
    got = back_in[...].astype(jnp.float32).reshape(2, nv, hb, LANES)
    grad[...] = jnp.sum(got, axis=1).reshape(2 * hb, LANES).astype(grad.dtype)

    wait(send_sems, 0, hid_in, hb)
    wait(send_sems, 1, rows, vb)
    wait(send_sems, 2, g_in, vb)
    wait(send_sems, 3, back_in, hb)


def local(nv, hid_student, teacher_logits, token_scale, head_student):
    tokens = 2 * nv
    depth, cols = head_student.shape
    hb = depth // LANES
    vb = cols // LANES
    f32, bf16 = jnp.float32, jnp.bfloat16
    vmem = pl.BlockSpec(memory_space=pltpu.VMEM)
    dma = pltpu.SemaphoreType.DMA
    loss, grad = pl.pallas_call(
        functools.partial(kernel, nv),
        out_shape=(
            jax.ShapeDtypeStruct((1, LANES), f32),
            jax.ShapeDtypeStruct((2 * hb, LANES), f32),
        ),
        in_specs=[vmem, vmem, vmem, pl.BlockSpec(memory_space=pltpu.HBM)],
        out_specs=(vmem, vmem),
        scratch_shapes=[
            pltpu.VMEM((depth, cols), bf16),
            pltpu.VMEM((tokens * hb, LANES), bf16),
            pltpu.VMEM((tokens * hb, LANES), f32),
            pltpu.VMEM((tokens * vb, LANES), f32),
            pltpu.VMEM((tokens * vb, LANES), f32),
            pltpu.VMEM((nv * vb, LANES), f32),
            pltpu.VMEM((tokens * vb, LANES), f32),
            pltpu.VMEM((tokens * hb, LANES), f32),
            pltpu.VMEM((tokens * hb, LANES), bf16),
            pltpu.VMEM((tokens * hb, LANES), bf16),
            dma((4,)),
            dma((4,)),
            dma((4,)),
        ],
        compiler_params=pltpu.CompilerParams(
            collective_id=0, has_side_effects=True, vmem_limit_bytes=48 * 1024 * 1024
        ),
    )(
        hid_student.reshape(2 * hb, LANES),
        teacher_logits.reshape(nv * vb, LANES),
        token_scale.reshape(1, 1),
        head_student,
    )
    return loss[0, :1], grad.astype(bf16).reshape(1, 2 * depth)


def solution(mesh):
    in_specs = (
        P(("groups", "vocab", "tok"), None),
        P(("groups", "vocab", "tok"), None),
        P(("groups", "vocab", "tok")),
        P("tok", "vocab"),
    )
    out_specs = (P(("groups", "vocab", "tok")), P(("groups", "vocab", "tok"), None))
    return jax.shard_map(
        functools.partial(local, mesh.shape["vocab"]),
        mesh=mesh,
        in_specs=in_specs,
        out_specs=out_specs,
        check_vma=False,
    )
```

```python
import functools
import math

import jax
import jax.numpy as jnp
from jax import lax
from jax.experimental import pallas as pl
from jax.experimental.pallas import tpu as pltpu
from jax.sharding import PartitionSpec as P

LANES = 128


def kernel(
    nv,
    hid,
    teach,
    scale,
    head,
    loss,
    grad,
    w,
    teach_v,
    hid_row,
    hid_32,
    hid_16,
    hid_in,
    hid_f,
    part,
    rows,
    g_out,
    g_in,
    back_f,
    back,
    back_in,
    w_sems,
    send_sems,
    recv_sems,
):
    tokens = 2 * nv
    depth, cols = head.shape
    hb = depth // LANES
    vb = cols // LANES
    v = lax.axis_index("vocab")
    t = lax.axis_index("tok")
    me = 2 * v + t
    slot = t * nv + v

    chunks = 4
    step = depth // chunks

    def w_copy(c):
        part_of = pl.ds(c * step, step)
        return pltpu.make_async_copy(head.at[part_of], w.at[part_of], w_sems.at[c])

    hid_copy = pltpu.make_async_copy(hid, hid_row, w_sems.at[chunks])
    teach_copy = pltpu.make_async_copy(teach, teach_v, w_sems.at[chunks + 1])
    hid_copy.start()
    teach_copy.start()
    for c in range(chunks):
        w_copy(c).start()

    def each_peer(fn):
        def one(k, _):
            peer = lax.rem(me + k, tokens)
            fn(peer, peer // 2, lax.rem(peer, 2))
            return 0

        lax.fori_loop(1, tokens, one, 0, unroll=tokens <= 16)

    barrier = pltpu.get_barrier_semaphore()

    def greet(peer, pv, pt):
        pl.semaphore_signal(barrier, inc=1, device_id={"vocab": pv, "tok": pt})

    each_peer(greet)
    hid_copy.wait()
    for r in range(2 * hb):
        lanes = slice(r * LANES, (r + 1) * LANES)
        hid_32[r : r + 1, :] = hid_row[:, lanes].astype(jnp.float32)
    hid_16[...] = hid_32[...].astype(jnp.bfloat16)
    pl.semaphore_wait(barrier, tokens - 1)

    def send(phase, src_of, dst):
        def one(peer, pv, pt):
            pltpu.make_async_remote_copy(
                src_ref=src_of(peer, pv, pt),
                dst_ref=dst,
                send_sem=send_sems.at[phase],
                recv_sem=recv_sems.at[phase],
                device_id={"vocab": pv, "tok": pt},
            ).start()

        each_peer(one)

    def wait(sems, phase, buf, block):
        ref = buf.at[pl.ds(0, (tokens - 1) * block)]
        pltpu.make_async_copy(ref, ref, sems.at[phase]).wait()

    def block(i, size):
        return pl.ds(pl.multiple_of(i * size, size), size)

    send(0, lambda p, pv, pt: hid_16.at[block(pt, hb)], hid_in.at[block(me, hb)])
    hid_in[block(me, hb), :] = hid_16[block(t, hb), :]

    teach_copy.wait()
    teacher = teach_v[...]
    top_t = jnp.max(teacher, keepdims=True)
    logq = teacher - (top_t + jnp.log(jnp.sum(jnp.exp(teacher - top_t), keepdims=True)))

    wait(recv_sems, 0, hid_in, hb)
    hid_f[...] = hid_in[...].astype(jnp.float32)
    x = jnp.concatenate(
        [hid_f[pl.ds(r, tokens, stride=hb), :].astype(jnp.bfloat16) for r in range(hb)], axis=1
    )
    for c in range(chunks):
        w_copy(c).wait()
    wide = 2 * LANES
    for c in range(cols // wide):
        y = jnp.dot(x, w[:, c * wide : (c + 1) * wide], preferred_element_type=jnp.float32)
        for h in range(2):
            part[pl.ds(2 * c + h, tokens, stride=vb), :] = y[:, h * LANES : (h + 1) * LANES]

    send(1, lambda p, pv, pt: part.at[block(p, vb)], rows.at[block(slot, vb)])
    rows[block(slot, vb), :] = part[block(me, vb), :]
    wait(recv_sems, 1, rows, vb)
    student = rows[0 : nv * vb, :] + rows[nv * vb : 2 * nv * vb, :]

    top_s = jnp.max(student, keepdims=True)
    logp = student - (top_s + jnp.log(jnp.sum(jnp.exp(student - top_s), keepdims=True)))
    logm = (
        jnp.maximum(logp, logq)
        + jnp.log1p(jnp.exp(-jnp.abs(logp - logq)))
        + jnp.float32(math.log(0.5))
    )
    prob_p = jnp.exp(logp)
    diff_p = logp - logm
    kl_p = jnp.sum(prob_p * diff_p, keepdims=True)
    weight = scale[...].astype(jnp.float32)
    g = (weight * prob_p * 0.5 * (diff_p - kl_p)).astype(jnp.bfloat16)
    g_out[...] = g.astype(jnp.float32)

    send(2, lambda p, pv, pt: g_out.at[block(pv, vb)], g_in.at[block(me, vb)])
    g_in[block(me, vb), :] = g_out[block(v, vb), :]
    kl_q = jnp.sum(jnp.exp(logq) * (logq - logm), keepdims=True)
    loss[...] = jnp.broadcast_to(0.5 * kl_p + 0.5 * kl_q, loss.shape)

    wait(recv_sems, 2, g_in, vb)
    gl = jnp.concatenate(
        [g_in[pl.ds(j, tokens, stride=vb), :].astype(jnp.bfloat16) for j in range(vb)], axis=1
    )
    for c in range(depth // wide):
        y = lax.dot_general(
            gl,
            w[c * wide : (c + 1) * wide, :],
            (((1,), (1,)), ((), ())),
            preferred_element_type=jnp.float32,
        )
        for h in range(2):
            back_f[pl.ds(2 * c + h, tokens, stride=hb), :] = y[:, h * LANES : (h + 1) * LANES]
    back[...] = back_f[...].astype(jnp.bfloat16)

    send(3, lambda p, pv, pt: back.at[block(p, hb)], back_in.at[block(slot, hb)])
    back_in[block(slot, hb), :] = back[block(me, hb), :]
    wait(recv_sems, 3, back_in, hb)
    got = back_in[...].astype(jnp.float32).reshape(2, nv, hb, LANES)
    hid_32[...] = jnp.sum(got, axis=1).reshape(2 * hb, LANES)
    for r in range(2 * hb):
        grad[:, r * LANES : (r + 1) * LANES] = hid_32[r : r + 1, :].astype(grad.dtype)

    wait(send_sems, 0, hid_in, hb)
    wait(send_sems, 1, rows, vb)
    wait(send_sems, 2, g_in, vb)
    wait(send_sems, 3, back_in, hb)


def local(nv, hid_student, teacher_logits, token_scale, head_student):
    tokens = 2 * nv
    depth, cols = head_student.shape
    hb = depth // LANES
    vb = cols // LANES
    f32, bf16 = jnp.float32, jnp.bfloat16
    vmem = pl.BlockSpec(memory_space=pltpu.VMEM)
    hbm = pl.BlockSpec(memory_space=pltpu.HBM)
    dma = pltpu.SemaphoreType.DMA
    loss, grad = pl.pallas_call(
        functools.partial(kernel, nv),
        out_shape=(
            jax.ShapeDtypeStruct((1, LANES), f32),
            jax.ShapeDtypeStruct((1, 2 * depth), bf16),
        ),
        in_specs=[hbm, hbm, vmem, hbm],
        out_specs=(vmem, vmem),
        scratch_shapes=[
            pltpu.VMEM((depth, cols), bf16),
            pltpu.VMEM((nv * vb, LANES), f32),
            pltpu.VMEM((1, 2 * depth), bf16),
            pltpu.VMEM((2 * hb, LANES), f32),
            pltpu.VMEM((2 * hb, LANES), bf16),
            pltpu.VMEM((tokens * hb, LANES), bf16),
            pltpu.VMEM((tokens * hb, LANES), f32),
            pltpu.VMEM((tokens * vb, LANES), f32),
            pltpu.VMEM((tokens * vb, LANES), f32),
            pltpu.VMEM((nv * vb, LANES), f32),
            pltpu.VMEM((tokens * vb, LANES), f32),
            pltpu.VMEM((tokens * hb, LANES), f32),
            pltpu.VMEM((tokens * hb, LANES), bf16),
            pltpu.VMEM((tokens * hb, LANES), bf16),
            dma((6,)),
            dma((4,)),
            dma((4,)),
        ],
        compiler_params=pltpu.CompilerParams(
            collective_id=0, has_side_effects=True, vmem_limit_bytes=60 * 1024 * 1024
        ),
    )(
        hid_student,
        teacher_logits.reshape(nv * vb, LANES),
        token_scale.reshape(1, 1),
        head_student,
    )
    return loss[0, :1], grad


def solution(mesh):
    in_specs = (
        P(("groups", "vocab", "tok"), None),
        P(("groups", "vocab", "tok"), None),
        P(("groups", "vocab", "tok")),
        P("tok", "vocab"),
    )
    out_specs = (P(("groups", "vocab", "tok")), P(("groups", "vocab", "tok"), None))
    return jax.shard_map(
        functools.partial(local, mesh.shape["vocab"]),
        mesh=mesh,
        in_specs=in_specs,
        out_specs=out_specs,
        check_vma=False,
    )
```

```python
import functools
import math

import jax
import jax.numpy as jnp
from jax import lax
from jax.experimental import pallas as pl
from jax.experimental.pallas import tpu as pltpu
from jax.sharding import PartitionSpec as P

LANES = 128


def kernel(
    nv,
    hid,
    teach,
    scale,
    head,
    loss,
    grad,
    w,
    teach_v,
    hid_row,
    hid_32,
    hid_16,
    hid_in,
    hid_f,
    logq_v,
    logq_in,
    part,
    other,
    norm_out,
    norm_in,
    back_f,
    back,
    back_in,
    stat,
    stat_in,
    w_sems,
    tok_sems,
    send_sems,
    recv_sems,
):
    tokens = 2 * nv
    depth, cols = head.shape
    hb = depth // LANES
    vb = cols // LANES
    v = lax.axis_index("vocab")
    t = lax.axis_index("tok")
    me = 2 * v + t
    slot = t * nv + v

    wide = 2 * LANES
    chunks = 4
    step = depth // chunks

    def w_copy(c):
        part_of = pl.ds(c * step, step)
        return pltpu.make_async_copy(head.at[part_of], w.at[part_of], w_sems.at[c])

    hid_copy = pltpu.make_async_copy(hid, hid_row, w_sems.at[chunks])
    teach_copy = pltpu.make_async_copy(teach, teach_v, w_sems.at[chunks + 1])
    hid_copy.start()
    teach_copy.start()
    for c in range(chunks):
        w_copy(c).start()

    def each_peer(fn):
        def one(k, _):
            peer = lax.rem(me + k, tokens)
            fn(peer, peer // 2, lax.rem(peer, 2))
            return 0

        lax.fori_loop(1, tokens, one, 0, unroll=tokens <= 16)

    barrier = pltpu.get_barrier_semaphore()

    def greet(peer, pv, pt):
        pl.semaphore_signal(barrier, inc=1, device_id={"vocab": pv, "tok": pt})

    each_peer(greet)
    hid_copy.wait()
    for r in range(2 * hb):
        lanes = slice(r * LANES, (r + 1) * LANES)
        hid_32[r : r + 1, :] = hid_row[:, lanes].astype(jnp.float32)
    hid_16[...] = hid_32[...].astype(jnp.bfloat16)
    teach_copy.wait()
    teacher = teach_v[...]
    top_t = jnp.max(teacher, keepdims=True)
    logq_v[...] = teacher - (
        top_t + jnp.log(jnp.sum(jnp.exp(teacher - top_t), keepdims=True))
    )
    pl.semaphore_wait(barrier, tokens - 1)

    def send(phase, src_of, dst):
        def one(peer, pv, pt):
            pltpu.make_async_remote_copy(
                src_ref=src_of(peer, pv, pt),
                dst_ref=dst,
                send_sem=send_sems.at[phase],
                recv_sem=recv_sems.at[phase],
                device_id={"vocab": pv, "tok": pt},
            ).start()

        each_peer(one)

    def wait(sems, phase, buf, block):
        ref = buf.at[pl.ds(0, (tokens - 1) * block)]
        pltpu.make_async_copy(ref, ref, sems.at[phase]).wait()

    def block(i, size):
        return pl.ds(pl.multiple_of(i * size, size), size)

    def tok_copy(c):
        part_of = pl.ds(c * wide, wide)
        return pltpu.make_async_remote_copy(
            src_ref=part.at[:, part_of],
            dst_ref=other.at[:, part_of],
            send_sem=tok_sems.at[0, c],
            recv_sem=tok_sems.at[1, c],
            device_id={"tok": 1 - t},
        )

    send(0, lambda p, pv, pt: hid_16.at[block(pt, hb)], hid_in.at[block(me, hb)])
    send(1, lambda p, pv, pt: logq_v.at[block(pv, vb)], logq_in.at[block(me, vb)])
    hid_in[block(me, hb), :] = hid_16[block(t, hb), :]
    logq_in[block(me, vb), :] = logq_v[block(v, vb), :]

    wait(recv_sems, 0, hid_in, hb)
    hid_f[...] = hid_in[...].astype(jnp.float32)
    x = jnp.concatenate(
        [hid_f[pl.ds(r, tokens, stride=hb), :].astype(jnp.bfloat16) for r in range(hb)], axis=1
    )
    for c in range(chunks):
        w_copy(c).wait()
    for c in range(cols // wide):
        part[:, c * wide : (c + 1) * wide] = jnp.dot(
            x, w[:, c * wide : (c + 1) * wide], preferred_element_type=jnp.float32
        )
        tok_copy(c).start()

    wait(recv_sems, 1, logq_in, vb)
    logq = jnp.concatenate([logq_in[pl.ds(j, tokens, stride=vb), :] for j in range(vb)], axis=1)
    for c in range(cols // wide):
        tok_copy(c).wait_recv()
    student = part[...] + other[...]

    top = jnp.max(student, axis=1, keepdims=True)
    norm = top + jnp.log(jnp.sum(jnp.exp(student - top), axis=1, keepdims=True))
    norm_out[...] = jnp.broadcast_to(norm, norm_out.shape)

    def send_norm(k, _):
        pv = lax.rem(v + k, nv)
        pltpu.make_async_remote_copy(
            src_ref=norm_out,
            dst_ref=norm_in.at[block(v, tokens)],
            send_sem=send_sems.at[2],
            recv_sem=recv_sems.at[2],
            device_id={"vocab": pv},
        ).start()
        return 0

    lax.fori_loop(1, nv, send_norm, 0, unroll=nv <= 8)
    norm_in[block(v, tokens), :] = norm_out[...]
    norms_ref = norm_in.at[pl.ds(0, (nv - 1) * tokens)]
    pltpu.make_async_copy(norms_ref, norms_ref, recv_sems.at[2]).wait()
    norms = norm_in[...].reshape(nv, tokens, LANES)
    peak = jnp.max(norms, axis=0)
    norm_all = peak + jnp.log(jnp.sum(jnp.exp(norms - peak[None]), axis=0))

    logp = student - norm_all[:, 0:1]
    logm = (
        jnp.maximum(logp, logq)
        + jnp.log1p(jnp.exp(-jnp.abs(logp - logq)))
        + jnp.float32(math.log(0.5))
    )
    prob_p = jnp.exp(logp)
    diff_p = logp - logm
    part_p = jnp.sum(prob_p * diff_p, axis=1, keepdims=True)
    mass = jnp.sum(prob_p, axis=1, keepdims=True)
    centre = part_p / jnp.maximum(mass, 1e-30)
    main = prob_p * (diff_p - centre)
    high = main.astype(jnp.bfloat16)
    low = (main - high.astype(jnp.float32)).astype(jnp.bfloat16)
    left = jnp.concatenate([high, low, prob_p.astype(jnp.bfloat16)], axis=0)
    for c in range(depth // wide):
        y = lax.dot_general(
            left,
            w[c * wide : (c + 1) * wide, :],
            (((1,), (1,)), ((), ())),
            preferred_element_type=jnp.float32,
        )
        moved = y[0:tokens] + y[tokens : 2 * tokens]
        mean = y[2 * tokens :]
        for h in range(2):
            lanes = slice(h * LANES, (h + 1) * LANES)
            back_f[pl.ds(2 * c + h, tokens, stride=2 * hb), :] = moved[:, lanes]
            back_f[pl.ds(hb + 2 * c + h, tokens, stride=2 * hb), :] = mean[:, lanes]
    back[...] = back_f[...].astype(jnp.bfloat16)

    part_q = jnp.sum(jnp.exp(logq) * (logq - logm), axis=1, keepdims=True)
    for r, column in enumerate((part_p, part_q, centre, centre)):
        stat[pl.ds(r, tokens, stride=8), :] = jnp.broadcast_to(column, (tokens, LANES))

    send(3, lambda p, pv, pt: back.at[block(p, 2 * hb)], back_in.at[block(slot, 2 * hb)])

    def four(i):
        return pl.ds(pl.multiple_of(i * 8, 8), 4)

    send(4, lambda p, pv, pt: stat.at[four(p)], stat_in.at[four(slot)])
    back_in[block(slot, 2 * hb), :] = back[block(me, 2 * hb), :]
    stat_in[four(slot), :] = stat[four(me), :]
    wait(recv_sems, 4, stat_in, 4)
    kl_p = jnp.sum(stat_in[pl.ds(0, tokens, stride=8), :][:nv], axis=0, keepdims=True)
    kl_q = jnp.sum(stat_in[pl.ds(1, tokens, stride=8), :][:nv], axis=0, keepdims=True)
    loss[...] = 0.5 * kl_p + 0.5 * kl_q
    shift = (kl_p - stat_in[pl.ds(2, tokens, stride=8), :]).reshape(tokens, 1, LANES)
    weight = 0.5 * scale[...].astype(jnp.float32)

    wait(recv_sems, 3, back_in, 2 * hb)
    got = back_in[...].astype(jnp.float32).reshape(tokens, 2, hb, LANES)
    terms = (got[:, 0] - shift * got[:, 1]).reshape(2, nv, hb, LANES)
    hid_32[...] = weight * jnp.sum(terms, axis=1).reshape(2 * hb, LANES)
    for r in range(2 * hb):
        grad[:, r * LANES : (r + 1) * LANES] = hid_32[r : r + 1, :].astype(grad.dtype)

    wait(send_sems, 0, hid_in, hb)
    wait(send_sems, 1, logq_in, vb)
    for c in range(cols // wide):
        tok_copy(c).wait_send()
    pltpu.make_async_copy(norms_ref, norms_ref, send_sems.at[2]).wait()
    wait(send_sems, 3, back_in, 2 * hb)
    wait(send_sems, 4, stat_in, 4)


def local(nv, hid_student, teacher_logits, token_scale, head_student):
    tokens = 2 * nv
    depth, cols = head_student.shape
    hb = depth // LANES
    vb = cols // LANES
    f32, bf16 = jnp.float32, jnp.bfloat16
    vmem = pl.BlockSpec(memory_space=pltpu.VMEM)
    hbm = pl.BlockSpec(memory_space=pltpu.HBM)
    dma = pltpu.SemaphoreType.DMA
    loss, grad = pl.pallas_call(
        functools.partial(kernel, nv),
        out_shape=(
            jax.ShapeDtypeStruct((1, LANES), f32),
            jax.ShapeDtypeStruct((1, 2 * depth), bf16),
        ),
        in_specs=[hbm, hbm, vmem, hbm],
        out_specs=(vmem, vmem),
        scratch_shapes=[
            pltpu.VMEM((depth, cols), bf16),
            pltpu.VMEM((nv * vb, LANES), f32),
            pltpu.VMEM((1, 2 * depth), bf16),
            pltpu.VMEM((2 * hb, LANES), f32),
            pltpu.VMEM((2 * hb, LANES), bf16),
            pltpu.VMEM((tokens * hb, LANES), bf16),
            pltpu.VMEM((tokens * hb, LANES), f32),
            pltpu.VMEM((nv * vb, LANES), f32),
            pltpu.VMEM((tokens * vb, LANES), f32),
            pltpu.VMEM((tokens, cols), f32),
            pltpu.VMEM((tokens, cols), f32),
            pltpu.VMEM((tokens, LANES), f32),
            pltpu.VMEM((nv * tokens, LANES), f32),
            pltpu.VMEM((tokens * 2 * hb, LANES), f32),
            pltpu.VMEM((tokens * 2 * hb, LANES), bf16),
            pltpu.VMEM((tokens * 2 * hb, LANES), bf16),
            pltpu.VMEM((tokens * 8, LANES), f32),
            pltpu.VMEM((tokens * 8, LANES), f32),
            dma((6,)),
            dma((2, cols // (2 * LANES))),
            dma((5,)),
            dma((5,)),
        ],
        compiler_params=pltpu.CompilerParams(
            collective_id=0, has_side_effects=True, vmem_limit_bytes=60 * 1024 * 1024
        ),
    )(
        hid_student,
        teacher_logits.reshape(nv * vb, LANES),
        token_scale.reshape(1, 1),
        head_student,
    )
    return loss[0, :1], grad


def solution(mesh):
    in_specs = (
        P(("groups", "vocab", "tok"), None),
        P(("groups", "vocab", "tok"), None),
        P(("groups", "vocab", "tok")),
        P("tok", "vocab"),
    )
    out_specs = (P(("groups", "vocab", "tok")), P(("groups", "vocab", "tok"), None))
    return jax.shard_map(
        functools.partial(local, mesh.shape["vocab"]),
        mesh=mesh,
        in_specs=in_specs,
        out_specs=out_specs,
        check_vma=False,
    )
```

```python
import functools
import math

import jax
import jax.numpy as jnp
from jax import lax
from jax.experimental import pallas as pl
from jax.experimental.pallas import tpu as pltpu
from jax.sharding import PartitionSpec as P

LANES = 128


def kernel(
    nv,
    hid,
    teach,
    scale,
    head,
    loss,
    grad,
    w,
    teach_v,
    hid_row,
    hid_32,
    hid_16,
    hid_in,
    hid_f,
    logq_v,
    logq_in,
    part,
    other,
    norm_out,
    norm_in,
    back_f,
    back,
    back_in,
    stat,
    stat_in,
    w_sems,
    tok_sems,
    send_sems,
    recv_sems,
):
    tokens = 2 * nv
    depth, cols = head.shape
    hb = depth // LANES
    vb = cols // LANES
    v = lax.axis_index("vocab")
    t = lax.axis_index("tok")
    me = 2 * v + t
    slot = t * nv + v

    wide = 2 * LANES
    chunks = 4
    step = depth // chunks

    def w_copy(c):
        part_of = pl.ds(c * step, step)
        return pltpu.make_async_copy(head.at[part_of], w.at[part_of], w_sems.at[c])

    hid_copy = pltpu.make_async_copy(hid, hid_row, w_sems.at[chunks])
    teach_copy = pltpu.make_async_copy(teach, teach_v, w_sems.at[chunks + 1])
    hid_copy.start()
    teach_copy.start()
    for c in range(chunks):
        w_copy(c).start()

    def each_peer(fn):
        def one(base, k):
            peer = base + lax.rem(me + k, nv)
            fn(peer, peer // 2, lax.rem(peer, 2))
            return base

        near = me // nv * nv
        lax.fori_loop(0, nv, lambda k, b: one(b, k), nv - near, unroll=nv <= 8)
        lax.fori_loop(1, nv, lambda k, b: one(b, k), near, unroll=nv <= 8)

    barrier = pltpu.get_barrier_semaphore()

    def greet(peer, pv, pt):
        pl.semaphore_signal(barrier, inc=1, device_id={"vocab": pv, "tok": pt})

    each_peer(greet)
    hid_copy.wait()
    for r in range(2 * hb):
        lanes = slice(r * LANES, (r + 1) * LANES)
        hid_32[r : r + 1, :] = hid_row[:, lanes].astype(jnp.float32)
    hid_16[...] = hid_32[...].astype(jnp.bfloat16)
    teach_copy.wait()
    teacher = teach_v[...]
    top_t = jnp.max(teacher, keepdims=True)
    logq_v[...] = teacher - (
        top_t + jnp.log(jnp.sum(jnp.exp(teacher - top_t), keepdims=True))
    )
    pl.semaphore_wait(barrier, tokens - 1)

    def send(phase, src_of, dst):
        def one(peer, pv, pt):
            pltpu.make_async_remote_copy(
                src_ref=src_of(peer, pv, pt),
                dst_ref=dst,
                send_sem=send_sems.at[phase],
                recv_sem=recv_sems.at[phase],
                device_id={"vocab": pv, "tok": pt},
            ).start()

        each_peer(one)

    def wait(sems, phase, buf, block):
        ref = buf.at[pl.ds(0, (tokens - 1) * block)]
        pltpu.make_async_copy(ref, ref, sems.at[phase]).wait()

    def block(i, size):
        return pl.ds(pl.multiple_of(i * size, size), size)

    def tok_copy(c):
        part_of = pl.ds(c * wide, wide)
        return pltpu.make_async_remote_copy(
            src_ref=part.at[:, part_of],
            dst_ref=other.at[:, part_of],
            send_sem=tok_sems.at[0, c],
            recv_sem=tok_sems.at[1, c],
            device_id={"tok": 1 - t},
        )

    send(0, lambda p, pv, pt: hid_16.at[block(pt, hb)], hid_in.at[block(me, hb)])
    hid_in[block(me, hb), :] = hid_16[block(t, hb), :]
    logq_in[block(me, vb), :] = logq_v[block(v, vb), :]

    wait(recv_sems, 0, hid_in, hb)
    hid_f[...] = hid_in[...].astype(jnp.float32)
    x = jnp.concatenate(
        [hid_f[pl.ds(r, tokens, stride=hb), :].astype(jnp.bfloat16) for r in range(hb)], axis=1
    )
    for c in range(chunks):
        w_copy(c).wait()
    for c in range(cols // wide):
        part[:, c * wide : (c + 1) * wide] = jnp.dot(
            x, w[:, c * wide : (c + 1) * wide], preferred_element_type=jnp.float32
        )
        tok_copy(c).start()
    send(1, lambda p, pv, pt: logq_v.at[block(pv, vb)], logq_in.at[block(me, vb)])

    for c in range(cols // wide):
        tok_copy(c).wait_recv()
    student = part[...] + other[...]

    top = jnp.max(student, axis=1, keepdims=True)
    norm = top + jnp.log(jnp.sum(jnp.exp(student - top), axis=1, keepdims=True))
    norm_out[...] = jnp.broadcast_to(norm, norm_out.shape)

    def send_norm(base, k):
        pv = base + lax.rem(v + k, half)
        pltpu.make_async_remote_copy(
            src_ref=norm_out,
            dst_ref=norm_in.at[block(v, tokens)],
            send_sem=send_sems.at[2],
            recv_sem=recv_sems.at[2],
            device_id={"vocab": pv},
        ).start()
        return base

    half = nv // 2
    close = v // half * half
    lax.fori_loop(0, half, lambda k, b: send_norm(b, k), half - close, unroll=nv <= 8)
    lax.fori_loop(1, half, lambda k, b: send_norm(b, k), close, unroll=nv <= 8)
    norm_in[block(v, tokens), :] = norm_out[...]
    wait(recv_sems, 1, logq_in, vb)
    logq = jnp.concatenate([logq_in[pl.ds(j, tokens, stride=vb), :] for j in range(vb)], axis=1)
    norms_ref = norm_in.at[pl.ds(0, (nv - 1) * tokens)]
    pltpu.make_async_copy(norms_ref, norms_ref, recv_sems.at[2]).wait()
    norms = norm_in[...].reshape(nv, tokens, LANES)
    peak = jnp.max(norms, axis=0)
    norm_all = peak + jnp.log(jnp.sum(jnp.exp(norms - peak[None]), axis=0))

    logp = student - norm_all[:, 0:1]
    logm = (
        jnp.maximum(logp, logq)
        + jnp.log1p(jnp.exp(-jnp.abs(logp - logq)))
        + jnp.float32(math.log(0.5))
    )
    prob_p = jnp.exp(logp)
    diff_p = logp - logm
    part_p = jnp.sum(prob_p * diff_p, axis=1, keepdims=True)
    mass = jnp.sum(prob_p, axis=1, keepdims=True)
    centre = part_p / jnp.maximum(mass, 1e-30)
    part_q = jnp.sum(jnp.exp(logq) * (logq - logm), axis=1, keepdims=True)
    for r, column in enumerate((part_p, part_q, centre, centre)):
        stat[pl.ds(r, tokens, stride=8), :] = jnp.broadcast_to(column, (tokens, LANES))

    def four(i):
        return pl.ds(pl.multiple_of(i * 8, 8), 4)

    send(4, lambda p, pv, pt: stat.at[four(p)], stat_in.at[four(slot)])
    stat_in[four(slot), :] = stat[four(me), :]

    main = prob_p * (diff_p - centre)
    high = main.astype(jnp.bfloat16)
    low = (main - high.astype(jnp.float32)).astype(jnp.bfloat16)
    left = jnp.concatenate([high, low, prob_p.astype(jnp.bfloat16)], axis=0)
    for c in range(depth // wide):
        y = lax.dot_general(
            left,
            w[c * wide : (c + 1) * wide, :],
            (((1,), (1,)), ((), ())),
            preferred_element_type=jnp.float32,
        )
        moved = y[0:tokens] + y[tokens : 2 * tokens]
        mean = y[2 * tokens :]
        for h in range(2):
            lanes = slice(h * LANES, (h + 1) * LANES)
            back_f[pl.ds(2 * c + h, tokens, stride=2 * hb), :] = moved[:, lanes]
            back_f[pl.ds(hb + 2 * c + h, tokens, stride=2 * hb), :] = mean[:, lanes]
    back[...] = back_f[...].astype(jnp.bfloat16)

    send(3, lambda p, pv, pt: back.at[block(p, 2 * hb)], back_in.at[block(slot, 2 * hb)])

    back_in[block(slot, 2 * hb), :] = back[block(me, 2 * hb), :]
    wait(recv_sems, 4, stat_in, 4)
    kl_p = jnp.sum(stat_in[pl.ds(0, tokens, stride=8), :][:nv], axis=0, keepdims=True)
    kl_q = jnp.sum(stat_in[pl.ds(1, tokens, stride=8), :][:nv], axis=0, keepdims=True)
    loss[...] = 0.5 * kl_p + 0.5 * kl_q
    shift = (kl_p - stat_in[pl.ds(2, tokens, stride=8), :]).reshape(tokens, 1, LANES)
    weight = 0.5 * scale[...].astype(jnp.float32)

    wait(recv_sems, 3, back_in, 2 * hb)
    got = back_in[...].astype(jnp.float32).reshape(tokens, 2, hb, LANES)
    terms = (got[:, 0] - shift * got[:, 1]).reshape(2, nv, hb, LANES)
    hid_32[...] = weight * jnp.sum(terms, axis=1).reshape(2 * hb, LANES)
    for r in range(2 * hb):
        grad[:, r * LANES : (r + 1) * LANES] = hid_32[r : r + 1, :].astype(grad.dtype)

    wait(send_sems, 0, hid_in, hb)
    wait(send_sems, 1, logq_in, vb)
    for c in range(cols // wide):
        tok_copy(c).wait_send()
    pltpu.make_async_copy(norms_ref, norms_ref, send_sems.at[2]).wait()
    wait(send_sems, 3, back_in, 2 * hb)
    wait(send_sems, 4, stat_in, 4)


def local(nv, hid_student, teacher_logits, token_scale, head_student):
    tokens = 2 * nv
    depth, cols = head_student.shape
    hb = depth // LANES
    vb = cols // LANES
    f32, bf16 = jnp.float32, jnp.bfloat16
    vmem = pl.BlockSpec(memory_space=pltpu.VMEM)
    hbm = pl.BlockSpec(memory_space=pltpu.HBM)
    dma = pltpu.SemaphoreType.DMA
    loss, grad = pl.pallas_call(
        functools.partial(kernel, nv),
        out_shape=(
            jax.ShapeDtypeStruct((1, LANES), f32),
            jax.ShapeDtypeStruct((1, 2 * depth), bf16),
        ),
        in_specs=[hbm, hbm, vmem, hbm],
        out_specs=(vmem, vmem),
        scratch_shapes=[
            pltpu.VMEM((depth, cols), bf16),
            pltpu.VMEM((nv * vb, LANES), f32),
            pltpu.VMEM((1, 2 * depth), bf16),
            pltpu.VMEM((2 * hb, LANES), f32),
            pltpu.VMEM((2 * hb, LANES), bf16),
            pltpu.VMEM((tokens * hb, LANES), bf16),
            pltpu.VMEM((tokens * hb, LANES), f32),
            pltpu.VMEM((nv * vb, LANES), f32),
            pltpu.VMEM((tokens * vb, LANES), f32),
            pltpu.VMEM((tokens, cols), f32),
            pltpu.VMEM((tokens, cols), f32),
            pltpu.VMEM((tokens, LANES), f32),
            pltpu.VMEM((nv * tokens, LANES), f32),
            pltpu.VMEM((tokens * 2 * hb, LANES), f32),
            pltpu.VMEM((tokens * 2 * hb, LANES), bf16),
            pltpu.VMEM((tokens * 2 * hb, LANES), bf16),
            pltpu.VMEM((tokens * 8, LANES), f32),
            pltpu.VMEM((tokens * 8, LANES), f32),
            dma((6,)),
            dma((2, cols // (2 * LANES))),
            dma((5,)),
            dma((5,)),
        ],
        compiler_params=pltpu.CompilerParams(
            collective_id=0, has_side_effects=True, vmem_limit_bytes=60 * 1024 * 1024
        ),
    )(
        hid_student,
        teacher_logits.reshape(nv * vb, LANES),
        token_scale.reshape(1, 1),
        head_student,
    )
    return loss[0, :1], grad


def solution(mesh):
    in_specs = (
        P(("groups", "vocab", "tok"), None),
        P(("groups", "vocab", "tok"), None),
        P(("groups", "vocab", "tok")),
        P("tok", "vocab"),
    )
    out_specs = (P(("groups", "vocab", "tok")), P(("groups", "vocab", "tok"), None))
    return jax.shard_map(
        functools.partial(local, mesh.shape["vocab"]),
        mesh=mesh,
        in_specs=in_specs,
        out_specs=out_specs,
        check_vma=False,
    )
```

```python
import functools
import math

import jax
import jax.numpy as jnp
from jax import lax
from jax.experimental import pallas as pl
from jax.experimental.pallas import tpu as pltpu
from jax.sharding import PartitionSpec as P

LANES = 128


def kernel(
    nv,
    hid,
    teach,
    scale,
    head,
    loss,
    grad,
    w,
    teach_v,
    hid_row,
    hid_32,
    hid_16,
    hid_in,
    hid_f,
    logq_v,
    logq_in,
    part,
    other,
    norm_out,
    norm_in,
    back_f,
    back,
    back_in,
    stat,
    stat_in,
    w_sems,
    tok_sems,
    send_sems,
    recv_sems,
):
    tokens = 2 * nv
    depth, cols = head.shape
    hb = depth // LANES
    vb = cols // LANES
    v = lax.axis_index("vocab")
    t = lax.axis_index("tok")
    me = 2 * v + t
    slot = t * nv + v

    wide = 2 * LANES
    chunks = 4
    step = depth // chunks

    def w_copy(c):
        part_of = pl.ds(c * step, step)
        return pltpu.make_async_copy(head.at[part_of], w.at[part_of], w_sems.at[c])

    hid_copy = pltpu.make_async_copy(hid, hid_row, w_sems.at[chunks])
    teach_copy = pltpu.make_async_copy(teach, teach_v, w_sems.at[chunks + 1])
    hid_copy.start()
    teach_copy.start()
    for c in range(chunks):
        w_copy(c).start()

    def each_peer(fn):
        def one(base, k):
            peer = base + lax.rem(me + k, nv)
            fn(peer, peer // 2, lax.rem(peer, 2))
            return base

        near = me // nv * nv
        lax.fori_loop(0, nv, lambda k, b: one(b, k), nv - near, unroll=nv <= 8)
        lax.fori_loop(1, nv, lambda k, b: one(b, k), near, unroll=nv <= 8)

    barrier = pltpu.get_barrier_semaphore()

    def greet(peer, pv, pt):
        pl.semaphore_signal(barrier, inc=1, device_id={"vocab": pv, "tok": pt})

    each_peer(greet)
    hid_copy.wait()
    for r in range(2 * hb):
        lanes = slice(r * LANES, (r + 1) * LANES)
        hid_32[r : r + 1, :] = hid_row[:, lanes].astype(jnp.float32)
    hid_16[...] = hid_32[...].astype(jnp.bfloat16)
    teach_copy.wait()
    teacher = teach_v[...]
    top_t = jnp.max(teacher, keepdims=True)
    logq_v[...] = teacher - (
        top_t + jnp.log(jnp.sum(jnp.exp(teacher - top_t), keepdims=True))
    )
    pl.semaphore_wait(barrier, tokens - 1)

    def send(phase, src_of, dst):
        def one(peer, pv, pt):
            pltpu.make_async_remote_copy(
                src_ref=src_of(peer, pv, pt),
                dst_ref=dst,
                send_sem=send_sems.at[phase],
                recv_sem=recv_sems.at[phase],
                device_id={"vocab": pv, "tok": pt},
            ).start()

        each_peer(one)

    def wait(sems, phase, buf, block):
        ref = buf.at[pl.ds(0, (tokens - 1) * block)]
        pltpu.make_async_copy(ref, ref, sems.at[phase]).wait()

    def block(i, size):
        return pl.ds(pl.multiple_of(i * size, size), size)

    def tok_copy(c):
        part_of = pl.ds(c * wide, wide)
        return pltpu.make_async_remote_copy(
            src_ref=part.at[:, part_of],
            dst_ref=other.at[:, part_of],
            send_sem=tok_sems.at[0, c],
            recv_sem=tok_sems.at[1, c],
            device_id={"tok": 1 - t},
        )

    send(0, lambda p, pv, pt: hid_16.at[block(pt, hb)], hid_in.at[block(me, hb)])
    hid_in[block(me, hb), :] = hid_16[block(t, hb), :]
    logq_in[block(me, vb), :] = logq_v[block(v, vb), :]

    wait(recv_sems, 0, hid_in, hb)
    hid_f[...] = hid_in[...].astype(jnp.float32)
    x = jnp.concatenate(
        [hid_f[pl.ds(r, tokens, stride=hb), :].astype(jnp.bfloat16) for r in range(hb)], axis=1
    )
    for c in range(chunks):
        w_copy(c).wait()
    for c in range(cols // wide):
        part[:, c * wide : (c + 1) * wide] = jnp.dot(
            x, w[:, c * wide : (c + 1) * wide], preferred_element_type=jnp.float32
        )
        tok_copy(c).start()
    send(1, lambda p, pv, pt: logq_v.at[block(pv, vb)], logq_in.at[block(me, vb)])

    for c in range(cols // wide):
        tok_copy(c).wait_recv()
    student = part[...] + other[...]

    top = jnp.max(student, axis=1, keepdims=True)
    norm = top + jnp.log(jnp.sum(jnp.exp(student - top), axis=1, keepdims=True))
    norm_out[...] = jnp.broadcast_to(norm, norm_out.shape)

    def send_norm(base, k):
        pv = base + lax.rem(v + k, half)
        pltpu.make_async_remote_copy(
            src_ref=norm_out,
            dst_ref=norm_in.at[block(v, tokens)],
            send_sem=send_sems.at[2],
            recv_sem=recv_sems.at[2],
            device_id={"vocab": pv},
        ).start()
        return base

    half = nv // 2
    close = v // half * half
    lax.fori_loop(0, half, lambda k, b: send_norm(b, k), half - close, unroll=nv <= 8)
    lax.fori_loop(1, half, lambda k, b: send_norm(b, k), close, unroll=nv <= 8)
    norm_in[block(v, tokens), :] = norm_out[...]
    wait(recv_sems, 1, logq_in, vb)
    logq = jnp.concatenate([logq_in[pl.ds(j, tokens, stride=vb), :] for j in range(vb)], axis=1)
    norms_ref = norm_in.at[pl.ds(0, (nv - 1) * tokens)]
    pltpu.make_async_copy(norms_ref, norms_ref, recv_sems.at[2]).wait()
    norms = norm_in[...].reshape(nv, tokens, LANES)
    peak = jnp.max(norms, axis=0)
    norm_all = peak + jnp.log(jnp.sum(jnp.exp(norms - peak[None]), axis=0))

    logp = student - norm_all[:, 0:1]
    logm = (
        jnp.maximum(logp, logq)
        + jnp.log1p(jnp.exp(-jnp.abs(logp - logq)))
        + jnp.float32(math.log(0.5))
    )
    prob_p = jnp.exp(logp)
    diff_p = logp - logm
    part_p = jnp.sum(prob_p * diff_p, axis=1, keepdims=True)
    mass = jnp.sum(prob_p, axis=1, keepdims=True)
    centre = part_p / jnp.maximum(mass, 1e-30)
    part_q = jnp.sum(jnp.exp(logq) * (logq - logm), axis=1, keepdims=True)
    for r, column in enumerate((part_p, part_q, centre, centre)):
        stat[pl.ds(r, tokens, stride=8), :] = jnp.broadcast_to(column, (tokens, LANES))

    def four(i):
        return pl.ds(pl.multiple_of(i * 8, 8), 4)

    send(4, lambda p, pv, pt: stat.at[four(p)], stat_in.at[four(slot)])
    stat_in[four(slot), :] = stat[four(me), :]

    main = prob_p * (diff_p - centre)
    high = main.astype(jnp.bfloat16)
    low = (main - high.astype(jnp.float32)).astype(jnp.bfloat16)
    left = jnp.concatenate([high, low, prob_p.astype(jnp.bfloat16)], axis=0)
    hh = hb // 2
    region = tokens * hb

    def send_back(part_no):
        def rows_of(i):
            return pl.ds(pl.multiple_of(part_no * region + i * hb, hb), hb)

        back[part_no * region : (part_no + 1) * region, :] = back_f[
            part_no * region : (part_no + 1) * region, :
        ].astype(jnp.bfloat16)
        phase = 3 + 2 * part_no
        send(phase, lambda p, pv, pt: back.at[rows_of(p)], back_in.at[rows_of(slot)])
        back_in[rows_of(slot), :] = back[rows_of(me), :]

    for c in range(depth // wide):
        y = lax.dot_general(
            left,
            w[c * wide : (c + 1) * wide, :],
            (((1,), (1,)), ((), ())),
            preferred_element_type=jnp.float32,
        )
        moved = y[0:tokens] + y[tokens : 2 * tokens]
        mean = y[2 * tokens :]
        for h in range(2):
            lanes = slice(h * LANES, (h + 1) * LANES)
            part_no, pos = divmod(2 * c + h, hh)
            row = part_no * region + pos
            back_f[pl.ds(row, tokens, stride=hb), :] = moved[:, lanes]
            back_f[pl.ds(row + hh, tokens, stride=hb), :] = mean[:, lanes]
        if (2 * c + 2) % hh == 0:
            send_back((2 * c + 1) // hh)

    wait(recv_sems, 4, stat_in, 4)
    kl_p = jnp.sum(stat_in[pl.ds(0, tokens, stride=8), :][:nv], axis=0, keepdims=True)
    kl_q = jnp.sum(stat_in[pl.ds(1, tokens, stride=8), :][:nv], axis=0, keepdims=True)
    loss[...] = 0.5 * kl_p + 0.5 * kl_q
    shift = (kl_p - stat_in[pl.ds(2, tokens, stride=8), :]).reshape(tokens, 1, LANES)
    weight = 0.5 * scale[...].astype(jnp.float32)

    for part_no in range(2):
        wait(recv_sems, 3 + 2 * part_no, back_in, hb)
        got = back_in[part_no * region : (part_no + 1) * region, :].astype(jnp.float32)
        got = got.reshape(tokens, 2, hh, LANES)
        terms = (got[:, 0] - shift * got[:, 1]).reshape(2, nv, hh, LANES)
        total = weight * jnp.sum(terms, axis=1)
        for r in range(2):
            hid_32[r * hb + part_no * hh : r * hb + (part_no + 1) * hh, :] = total[r]
    for r in range(2 * hb):
        grad[:, r * LANES : (r + 1) * LANES] = hid_32[r : r + 1, :].astype(grad.dtype)

    wait(send_sems, 0, hid_in, hb)
    wait(send_sems, 1, logq_in, vb)
    for c in range(cols // wide):
        tok_copy(c).wait_send()
    pltpu.make_async_copy(norms_ref, norms_ref, send_sems.at[2]).wait()
    wait(send_sems, 3, back_in, hb)
    wait(send_sems, 5, back_in, hb)
    wait(send_sems, 4, stat_in, 4)


def local(nv, hid_student, teacher_logits, token_scale, head_student):
    tokens = 2 * nv
    depth, cols = head_student.shape
    hb = depth // LANES
    vb = cols // LANES
    f32, bf16 = jnp.float32, jnp.bfloat16
    vmem = pl.BlockSpec(memory_space=pltpu.VMEM)
    hbm = pl.BlockSpec(memory_space=pltpu.HBM)
    dma = pltpu.SemaphoreType.DMA
    loss, grad = pl.pallas_call(
        functools.partial(kernel, nv),
        out_shape=(
            jax.ShapeDtypeStruct((1, LANES), f32),
            jax.ShapeDtypeStruct((1, 2 * depth), bf16),
        ),
        in_specs=[hbm, hbm, vmem, hbm],
        out_specs=(vmem, vmem),
        scratch_shapes=[
            pltpu.VMEM((depth, cols), bf16),
            pltpu.VMEM((nv * vb, LANES), f32),
            pltpu.VMEM((1, 2 * depth), bf16),
            pltpu.VMEM((2 * hb, LANES), f32),
            pltpu.VMEM((2 * hb, LANES), bf16),
            pltpu.VMEM((tokens * hb, LANES), bf16),
            pltpu.VMEM((tokens * hb, LANES), f32),
            pltpu.VMEM((nv * vb, LANES), f32),
            pltpu.VMEM((tokens * vb, LANES), f32),
            pltpu.VMEM((tokens, cols), f32),
            pltpu.VMEM((tokens, cols), f32),
            pltpu.VMEM((tokens, LANES), f32),
            pltpu.VMEM((nv * tokens, LANES), f32),
            pltpu.VMEM((tokens * 2 * hb, LANES), f32),
            pltpu.VMEM((tokens * 2 * hb, LANES), bf16),
            pltpu.VMEM((tokens * 2 * hb, LANES), bf16),
            pltpu.VMEM((tokens * 8, LANES), f32),
            pltpu.VMEM((tokens * 8, LANES), f32),
            dma((6,)),
            dma((2, cols // (2 * LANES))),
            dma((6,)),
            dma((6,)),
        ],
        compiler_params=pltpu.CompilerParams(
            collective_id=0, has_side_effects=True, vmem_limit_bytes=60 * 1024 * 1024
        ),
    )(
        hid_student,
        teacher_logits.reshape(nv * vb, LANES),
        token_scale.reshape(1, 1),
        head_student,
    )
    return loss[0, :1], grad


def solution(mesh):
    in_specs = (
        P(("groups", "vocab", "tok"), None),
        P(("groups", "vocab", "tok"), None),
        P(("groups", "vocab", "tok")),
        P("tok", "vocab"),
    )
    out_specs = (P(("groups", "vocab", "tok")), P(("groups", "vocab", "tok"), None))
    return jax.shard_map(
        functools.partial(local, mesh.shape["vocab"]),
        mesh=mesh,
        in_specs=in_specs,
        out_specs=out_specs,
        check_vma=False,
    )
```
